32 devices in a mesh: groups: 2 (over x), eigen: 16 (over z, y, core).
Axes of the slice: x: 2, y: 2, z: 4, core: 2. Of those that a mesh axis runs over, the one named last changes fastest.
Arguments:
- acts: bfloat16 [64, 8192], P(('groups', 'eigen')), parts along dimension 0, may hold values from -6 to 6
- grads: bfloat16 [64, 8192], P(('groups', 'eigen')), parts along dimension 0, may hold values from -0.75 to 0.75
- lengths: int32 [8], P('groups'), parts along dimension 0, may hold values from 1 to 16, 32 in all
- basis_in: float32 [16384, 8192], P('groups', 'eigen'), parts along dimension 0
- basis_out: float32 [16384, 8192], P('groups', 'eigen'), parts along dimension 0
Outputs:
- corrections: float32 [16384, 8192], P('groups', 'eigen'), parts along dimension 0
- precond: float32 [256, 8192], P('groups', 'eigen'), parts along dimension 0
The draws below stay inside these ranges and needn't reach their ends.
There are 2 independent parts, one for each index of `groups`. The reference program is written for one: setup_inputs(seed, part) draws one part's arguments, and reference() takes and returns one part's arrays. A program takes and returns all parts, laid end to end along the dimension named above; each array names one. Nothing has to cross between parts.
Inputs may be any that keep to these rules, and one draw needn't show every extreme that they name: The lengths sum to 32; the longest is exactly 16.
All inputs are finite; a program needn't handle non-finite values.
Results may differ from the reference program's by a relative error of at most 0.0066.
Values may be sent and summed in bfloat16 or wider, within the bound.
A program may use at most 192 MiB of HBM per device.

```python
import math
import jax
import jax.numpy as jnp
import numpy as np
from jax import lax

D_IN = 8192
D_OUT = 8192
SEQS = 4
OUT_ROWS = 128
TOKENS = 32


def scale_columns(key, base, rows, cols):
    where = jnp.arange(cols, dtype=jnp.float32) / cols
    factor = jax.random.uniform(key, (cols,), jnp.float32, 0.5, 2.0)
    spread = jnp.exp(where * jnp.log(4.0)) * factor
    return base * spread[None, :] / jnp.sqrt(jnp.float32(rows))


def draw_basis_in(key, part):
    key = jax.random.fold_in(key, 11)
    key_base, key_cols = jax.random.split(key)
    base = jax.random.normal(key_base, (D_IN, D_IN), jnp.float32)
    return scale_columns(key_cols, base, D_IN, D_IN)


def draw_basis_out(key, part):
    key = jax.random.fold_in(key, 23)
    key_base, key_cols = jax.random.split(key)
    base = jax.random.normal(key_base, (D_OUT, D_OUT), jnp.float32)
    return scale_columns(key_cols, base, D_OUT, D_OUT)


def block_levels(own_key, extent, cuts, smallest, high):
    factor_of = 1.0
    for dim, parts in cuts:
        steps = jax.random.uniform(jax.random.fold_in(jax.random.fold_in(own_key, 6), dim), (parts,), jnp.float32, smallest / len(cuts), high / len(cuts))
        factor_of = factor_of * jnp.repeat(jnp.exp(steps), extent[dim] // parts).reshape((-1,) + (1,) * (len(extent) - 1 - dim))
    return factor_of


def split_up(number_of, total, bound, lean):
    portions = [(1 << 20) // math.isqrt(grade ** lean) + 1 for grade in range(2, number_of + 1)]
    spare, holding = total - bound - (number_of - 1), [1] * (number_of - 1)
    while spare > 0:
        candidates = [i for i in range(number_of - 1) if holding[i] < bound]
        whole, budget = sum([portions[i] for i in candidates]), spare
        for i in candidates:
            more = min(bound - holding[i], max(1, budget * portions[i] // whole), spare)
            holding[i] = holding[i] + more
            spare = spare - more
    return np.array([bound] + holding)


def ragged(stream_key, number_of, total, reach, lean):
    if number_of == 2:
        one = jax.random.randint(stream_key, (), max(1, total - reach), min(reach, total - 1) + 1)
        return jnp.stack([one, total - one])
    sizes = jnp.asarray(split_up(number_of, total, reach, lean), jnp.int32)
    pairs = (number_of - 1) // 2
    giver, sink = sizes[1:1 + 2 * pairs:2], sizes[2:2 + 2 * pairs:2]
    slack = jnp.minimum(giver - 1, reach - sink)
    shifted = jax.random.randint(jax.random.fold_in(stream_key, 1), (pairs,), 0, 1 << 20) % (slack + 1)
    sizes = sizes.at[1:1 + 2 * pairs:2].set(giver - shifted).at[2:2 + 2 * pairs:2].set(sink + shifted)
    return sizes[jax.random.permutation(jax.random.fold_in(stream_key, 2), number_of)]


def centred(stream_key, shape, deviation, most, shards=(), held_as=jnp.bfloat16):
    values = jax.random.normal(stream_key, shape, jnp.float32) * deviation
    if len(shards) > 0:
        values = block_levels(stream_key, shape, shards, -0.22, 0.18) * values
    return jnp.clip(values, min=-most, max=most).astype(held_as)


def setup_inputs(seed: int = 0, part: int = 0) -> dict:
    arg_keys = jax.random.split(jax.random.key(seed), 6)
    part_splits = jax.random.split(jax.random.fold_in(arg_keys[5], part), 6)
    acts = centred(part_splits[0], (TOKENS, D_IN), 1.0, 6.0, ((0, 16),))
    grads = centred(part_splits[1], (TOKENS, D_OUT), 0.125, 0.75, ((0, 16),))
    lengths = ragged(part_splits[2], SEQS, TOKENS, TOKENS // 2, 2).astype(jnp.int32)
    basis_in = draw_basis_in(jax.random.fold_in(jax.random.fold_in(arg_keys[5], part), 71), part)
    basis_out = draw_basis_out(jax.random.fold_in(jax.random.fold_in(arg_keys[5], part), 71), part)
    return {"acts": acts, "grads": grads, "lengths": lengths, "basis_in": basis_in, "basis_out": basis_out}


damp_share = 0.1


def reference(acts, grads, lengths, basis_in, basis_out):
    highest = lax.Precision.HIGHEST
    rot_in = jnp.dot(acts.astype(jnp.float32), basis_in, precision=highest, preferred_element_type=jnp.float32).astype(jnp.bfloat16)
    rot_out = jnp.dot(grads.astype(jnp.float32), basis_out, precision=highest, preferred_element_type=jnp.float32).astype(jnp.bfloat16)
    ends = jnp.cumsum(lengths).astype(jnp.int32)
    starts = ends - lengths.astype(jnp.int32)
    position = jnp.arange(TOKENS, dtype=jnp.int32)
    total = jnp.zeros((D_OUT, D_IN), jnp.float32)
    squares = jnp.zeros((D_OUT, D_IN), jnp.float32)
    for seq_id in range(SEQS):
        inside = ((position >= starts[seq_id]) & (position < ends[seq_id])).astype(jnp.bfloat16)
        masked = rot_in * inside[:, None]
        product = jnp.dot(rot_out.T, masked, preferred_element_type=jnp.float32)
        total = total + product
        squares = squares + product * product
    corrections = squares / SEQS
    mean_rot = total / SEQS
    damping = damp_share * jnp.mean(corrections)
    scaled = mean_rot / (corrections + damping)
    left_part = jnp.dot(basis_out[:OUT_ROWS, :], scaled, precision=highest, preferred_element_type=jnp.float32)
    precond = jnp.dot(left_part, basis_in.T, precision=highest, preferred_element_type=jnp.float32)
    return corrections, precond
```

```python
import functools

import jax
import jax.numpy as jnp
from jax import lax
from jax.experimental import pallas as pl
from jax.experimental.pallas import tpu as pltpu
from jax.sharding import PartitionSpec as P

SEQS = 4
OUT_ROWS = 128
CORES = 2
ROW_TILE = 16
damp_share = 0.1
BF16 = jnp.bfloat16
F32 = jnp.float32
VMEM_BYTES = 56 * 1024 * 1024


def grid_of(n):
    wide = 2 if n <= 16 else 1
    return n // (CORES * wide), wide


class Place:
    def __init__(self, n):
        self.n = n
        self.depth, self.wide = grid_of(n)
        self.me = lax.axis_index("eigen")
        self.core = lax.rem(self.me, CORES)
        self.y = lax.rem(self.me // CORES, self.wide)
        self.z = self.me // (CORES * self.wide)

    def at(self, z, y, core):
        return (z * self.wide + y) * CORES + core


def entry_barrier(place):
    barrier = pltpu.get_barrier_semaphore()
    for step in range(1, place.n):
        other = lax.rem(place.me + step, place.n)
        pl.semaphore_signal(
            barrier, inc=1, device_id={"eigen": other}, device_id_type=pl.DeviceIdType.MESH
        )
    pl.semaphore_wait(barrier, place.n - 1)


def remote(src, dst, send_sem, recv_sem, to):
    return pltpu.make_async_remote_copy(
        src_ref=src,
        dst_ref=dst,
        send_sem=send_sem,
        recv_sem=recv_sem,
        device_id={"eigen": to},
        device_id_type=pl.DeviceIdType.MESH,
    )


class Gather:
    def __init__(self, place, slots, send_sems, recv_sems):
        self.p, self.slots = place, slots
        self.send_sems, self.recv_sems = send_sems, recv_sems

    def copy(self, slot, way, to):
        return remote(
            self.slots.at[slot],
            self.slots.at[slot],
            self.send_sems.at[way, slot],
            self.recv_sems.at[slot],
            to,
        )

    def arrived(self, slot):
        self.copy(slot, 0, self.p.me).wait_recv()

    def up(self, slot, act):
        p = self.p

        @pl.when(p.z < p.depth - 1)
        def _():
            act(self.copy(slot, 0, p.at(p.z + 1, p.y, p.core)))

    def down(self, slot, act):
        p = self.p

        @pl.when(p.z > 0)
        def _():
            act(self.copy(slot, 1, p.at(p.z - 1, p.y, p.core)))

    def across(self, slot, act):
        p = self.p
        if p.wide > 1:
            act(self.copy(slot, 2, p.at(p.z, 1 - p.y, p.core)))
        self.over(slot, act)

    def over(self, slot, act):
        p = self.p
        act(self.copy(slot, 3, p.at(p.z, p.y, 1 - p.core)))

    def beside(self, dz):
        p = self.p
        if p.wide > 1:
            slot = p.at(p.z + dz, 1 - p.y, p.core)
            self.arrived(slot)
            self.over(slot, start)

    def round(self, h):
        p = self.p
        if h == 0:
            self.up(p.me, start)
            self.down(p.me, start)
            self.across(p.me, start)
            return

        @pl.when(p.z - h >= 0)
        def _():
            slot = p.at(p.z - h, p.y, p.core)
            self.arrived(slot)
            self.up(slot, start)
            self.across(slot, start)

        @pl.when(p.z + h < p.depth)
        def _():
            slot = p.at(p.z + h, p.y, p.core)
            self.arrived(slot)
            self.down(slot, start)
            self.across(slot, start)

        self.beside_round(h - 1)

    def beside_round(self, h):
        p = self.p
        if h == 0:
            self.beside(0)
            return

        @pl.when(p.z - h >= 0)
        def _():
            self.beside(-h)

        @pl.when(p.z + h < p.depth)
        def _():
            self.beside(h)

    def last(self):
        p = self.p
        self.beside_round(p.depth - 1)
        for z in range(p.depth):
            for y in range(p.wide):
                self.arrived(p.at(z, y, 1 - p.core))

    def drain(self):
        p = self.p
        for z in range(p.depth):
            slot = p.at(z, p.y, p.core)

            @pl.when(z <= p.z)
            def _():
                self.up(slot, wait_send)

            @pl.when(z >= p.z)
            def _():
                self.down(slot, wait_send)

            self.across(slot, wait_send)
            if p.wide > 1:
                self.over(p.at(z, 1 - p.y, p.core), wait_send)


def start(copy):
    copy.start()


def wait_send(copy):
    copy.wait_send()


def sequence_ends(lengths):
    ends, total = [], 0
    for s in range(SEQS):
        total = total + lengths[s]
        ends.append(total)
    return ends


def sequence_of(position, ends):
    which = jnp.zeros(position.shape, jnp.int32)
    for s in range(SEQS - 1):
        which = which + (position >= ends[s]).astype(jnp.int32)
    return which


def rotate_kernel(
    n,
    rows_ref,
    lengths,
    basis_in,
    basis_out,
    rot_out_hbm,
    window_hbm,
    rot_in_ref,
    damp_ref,
    held,
    tokens,
    window_f32,
    window,
    rot_out,
    parts,
    acc,
    held_sems,
    token_send,
    token_recv,
    window_send,
    window_recv,
    rot_send,
    rot_recv,
    part_send,
    part_recv,
    local_sems,
):
    place = Place(n)
    features, width = basis_in.shape
    steps = held.shape[1]
    chunk = features // steps
    count = rot_in_ref.shape[0]

    def load(which, k):
        source = basis_out if which == 0 else basis_in
        return pltpu.make_async_copy(
            source.at[pl.ds(k * chunk, chunk)], held.at[which, k], held_sems.at[which, k]
        )

    first_rows = pltpu.make_async_copy(
        basis_out.at[pl.ds(0, OUT_ROWS)], window_f32, local_sems.at[0]
    )
    first_rows.start()
    for which in range(2):
        for k in range(steps):
            load(which, k).start()

    tokens[place.me] = rows_ref[...]
    entry_barrier(place)
    token_gather = Gather(place, tokens, token_send, token_recv)
    window_gather = Gather(place, window, window_send, window_recv)
    rot_gather = Gather(place, rot_out, rot_send, rot_recv)
    for h in range(place.depth):
        token_gather.round(h)
    token_gather.last()
    first_rows.wait()
    window[place.me] = window_f32[...].astype(BF16)
    window_gather.round(0)

    def rotate(which, low, high):
        row = lax.broadcasted_iota(jnp.int32, (count, n * ROW_TILE), 0)
        col = lax.broadcasted_iota(jnp.int32, (count, n * ROW_TILE), 1)
        here = pl.ds((1 - which) * ROW_TILE, ROW_TILE)
        flat = tokens[:, here, :].reshape(n * ROW_TILE, chunk)

        def body(k, carry):
            load(which, k).wait()
            pick = (col == row * steps + k).astype(F32).astype(BF16)
            left = jnp.dot(pick, flat, preferred_element_type=F32).astype(BF16)
            block = held[which, k]
            high_part = block.astype(BF16)
            low_part = (block - high_part.astype(F32)).astype(BF16)
            acc[...] += jnp.dot(left, high_part, preferred_element_type=F32) + jnp.dot(
                left, low_part, preferred_element_type=F32
            )
            return carry

        lax.fori_loop(low, high, body, 0)

    half = steps // 2
    rounds = list(range(1, place.depth))
    acc[...] = jnp.zeros_like(acc)
    rotate(0, 0, half)
    for h in rounds[:1]:
        window_gather.round(h)
    rotate(0, half, steps)
    rot_out[place.me] = acc[...].astype(BF16)
    rot_gather.round(0)
    for h in rounds[1:2]:
        window_gather.round(h)
    acc[...] = jnp.zeros_like(acc)
    rotate(1, 0, half)
    for h in rounds[:1]:
        rot_gather.round(h)
    for h in rounds[2:]:
        window_gather.round(h)
    rotate(1, half, steps)
    rot_in = acc[...].astype(BF16)
    rot_in_ref[...] = rot_in
    for h in rounds[1:]:
        rot_gather.round(h)
    rot_gather.last()

    contract = (((1,), (1,)), ((), ()))
    gram_in = lax.dot_general(rot_in, rot_in, contract, preferred_element_type=F32)
    gram_out = jnp.zeros((count, count), F32)
    for d in range(n):
        gram_out += lax.dot_general(rot_out[d], rot_out[d], contract, preferred_element_type=F32)
    ends = sequence_ends(lengths)
    one = sequence_of(lax.broadcasted_iota(jnp.int32, (count, count), 0), ends)
    two = sequence_of(lax.broadcasted_iota(jnp.int32, (count, count), 1), ends)
    inner = jnp.sum(jnp.where(one == two, gram_in * gram_out, 0.0))
    parts[place.me] = jnp.full(parts.shape[1:], inner, F32)

    def part_copy(step):
        other = lax.rem(place.me + step, n)
        return remote(
            parts.at[place.me],
            parts.at[place.me],
            part_send.at[step],
            part_recv.at[place.me],
            other,
        )

    for step in range(1, n):
        part_copy(step).start()
    out_copy = pltpu.make_async_copy(rot_out, rot_out_hbm, local_sems.at[1])
    out_copy.start()
    window_gather.last()
    window_copy = pltpu.make_async_copy(window, window_hbm, local_sems.at[2])
    window_copy.start()
    for step in range(1, n):
        other = lax.rem(place.me + step, n)
        remote(
            parts.at[other], parts.at[other], part_send.at[step], part_recv.at[other], other
        ).wait_recv()
    total = jnp.sum(parts[...], axis=0)
    damp_ref[...] = total * (damp_share / (SEQS * features * (n * width)))
    for step in range(1, n):
        part_copy(step).wait_send()
    token_gather.drain()
    window_gather.drain()
    rot_gather.drain()
    out_copy.wait()
    window_copy.wait()


def rotate_all(n, rows, lengths, basis_in, basis_out):
    features, width = basis_in.shape
    chunk = rows.shape[1]
    steps = features // chunk
    count = n * ROW_TILE // steps
    sems = pltpu.SemaphoreType.DMA
    return pl.pallas_call(
        functools.partial(rotate_kernel, n),
        out_shape=(
            jax.ShapeDtypeStruct((n, count, width), BF16),
            jax.ShapeDtypeStruct((n, OUT_ROWS, width), BF16),
            jax.ShapeDtypeStruct((count, width), BF16),
            jax.ShapeDtypeStruct((8, 128), F32),
        ),
        in_specs=[
            pl.BlockSpec(memory_space=pltpu.VMEM),
            pl.BlockSpec(memory_space=pltpu.SMEM),
            pl.BlockSpec(memory_space=pl.ANY),
            pl.BlockSpec(memory_space=pl.ANY),
        ],
        out_specs=(
            pl.BlockSpec(memory_space=pl.ANY),
            pl.BlockSpec(memory_space=pl.ANY),
            pl.BlockSpec(memory_space=pltpu.VMEM),
            pl.BlockSpec(memory_space=pltpu.VMEM),
        ),
        scratch_shapes=[
            pltpu.VMEM((2, steps, chunk, width), F32),
            pltpu.VMEM((n, 2 * ROW_TILE, chunk), BF16),
            pltpu.VMEM((OUT_ROWS, width), F32),
            pltpu.VMEM((n, OUT_ROWS, width), BF16),
            pltpu.VMEM((n, count, width), BF16),
            pltpu.VMEM((n, 8, 128), F32),
            pltpu.VMEM((count, width), F32),
            sems((2, steps)),
            sems((4, n)),
            sems((n,)),
            sems((4, n)),
            sems((n,)),
            sems((4, n)),
            sems((n,)),
            sems((n,)),
            sems((n,)),
            sems((3,)),
        ],
        compiler_params=pltpu.CompilerParams(
            collective_id=0, has_side_effects=True, vmem_limit_bytes=VMEM_BYTES
        ),
        name="rotate_and_gather",
    )(rows, lengths, basis_in, basis_out)


def correct_kernel(lengths, rot_out, window, rot_in, damp, corrections, left, masked):
    block = pl.program_id(0)
    count, width = rot_in.shape

    @pl.when(block == 0)
    def _():
        which = sequence_of(
            lax.broadcasted_iota(jnp.int32, (count, width), 0), sequence_ends(lengths)
        )
        half = rot_in[...].astype(F32) * 0.5
        for s in range(SEQS):
            masked[:, s * width : (s + 1) * width] = jnp.where(which == s, half, 0.0).astype(BF16)
        left[...] = jnp.zeros_like(left)

    columns = rot_out[0].astype(F32).T.astype(BF16)
    tile = 64
    damping = damp[0:1, 0:1]
    scaled = []
    for low in range(0, columns.shape[0], tile):
        rows = columns[low : low + tile]
        squares, total = None, None
        for s in range(SEQS):
            product = jnp.dot(
                rows, masked[:, s * width : (s + 1) * width], preferred_element_type=F32
            )
            squares = product * product if s == 0 else squares + product * product
            total = product if s == 0 else total + product
        corrections[low : low + tile, :] = squares
        scaled.append((total / (squares + damping)).astype(BF16))
    left[...] += jnp.dot(window[0], jnp.concatenate(scaled, 0), preferred_element_type=F32)

    @pl.when(block == pl.num_programs(0) - 1)
    def _():
        left[...] = left[...] * 0.5


def correct(lengths, rot_out, window, rot_in, damp):
    n, count, width = rot_out.shape
    whole = lambda i: (0, 0)
    return pl.pallas_call(
        correct_kernel,
        grid=(n,),
        out_shape=(
            jax.ShapeDtypeStruct((n * width, width), F32),
            jax.ShapeDtypeStruct((OUT_ROWS, width), F32),
        ),
        in_specs=[
            pl.BlockSpec(memory_space=pltpu.SMEM),
            pl.BlockSpec((1, count, width), lambda i: (i, 0, 0)),
            pl.BlockSpec((1, OUT_ROWS, width), lambda i: (i, 0, 0)),
            pl.BlockSpec((count, width), whole),
            pl.BlockSpec((8, 128), whole),
        ],
        out_specs=(
            pl.BlockSpec((width, width), lambda i: (i, 0)),
            pl.BlockSpec((OUT_ROWS, width), whole),
        ),
        scratch_shapes=[pltpu.VMEM((count, SEQS * width), BF16)],
        compiler_params=pltpu.CompilerParams(vmem_limit_bytes=VMEM_BYTES),
        name="corrections",
    )(lengths, rot_out, window, rot_in, damp)


def back_kernel(
    n,
    left_ref,
    basis,
    out,
    held,
    own,
    core_out,
    core_in,
    y_out,
    y_in,
    z_out,
    from_below,
    from_above,
    held_sems,
    core_send,
    core_recv,
    y_send,
    y_recv,
    z_send,
    below_recv,
    above_recv,
):
    place = Place(n)
    p = place
    width = basis.shape[1]

    def load(d):
        return pltpu.make_async_copy(
            basis.at[pl.ds(pl.multiple_of(d * width, width), width)], held.at[d], held_sems.at[d]
        )

    def in_order(visit):
        for h in range(p.depth - 1, 0, -1):
            for there in (p.z + h, p.z - h):

                @pl.when((there >= 0) & (there < p.depth))
                def _():
                    visit(there)

        visit(p.z)

    def load_all(z):
        for y in range(p.wide):
            for core in range(CORES):
                load(p.at(z, y, core)).start()

    in_order(load_all)
    left = left_ref[...].astype(BF16)
    entry_barrier(place)

    def partial_of(z, y, core):
        d = p.at(z, y, core)
        load(d).wait()
        return lax.dot_general(
            left, held[d].astype(BF16), (((1,), (1,)), ((), ())), preferred_element_type=F32
        )

    sides = [1, 0] if p.wide > 1 else [0]

    def core_copy(z, side):
        k = z * p.wide + side
        return remote(
            core_out.at[k],
            core_in.at[k],
            core_send.at[k],
            core_recv.at[k],
            p.at(p.z, p.y, 1 - p.core),
        )

    def y_copy(z):
        return remote(
            y_out.at[z], y_in.at[z], y_send.at[z], y_recv.at[z], p.at(p.z, 1 - p.y, p.core)
        )

    def up_copy(z):
        return remote(
            z_out.at[z], from_below.at[z], z_send.at[z], below_recv.at[z],
            p.at(p.z + 1, p.y, p.core),
        )

    def down_copy(z):
        return remote(
            z_out.at[z], from_above.at[z], z_send.at[z], above_recv.at[z],
            p.at(p.z - 1, p.y, p.core),
        )

    def compute(z):
        for side in sides:
            y = 1 - p.y if side == 1 else p.y
            k = z * p.wide + side
            core_out[k] = partial_of(z, y, 1 - p.core).astype(BF16)
            core_copy(z, side).start()
        for side in sides:
            y = 1 - p.y if side == 1 else p.y
            own[z * p.wide + side] = partial_of(z, y, p.core)

    def pair(z):
        for side in sides:
            k = z * p.wide + side
            core_copy(z, side).wait_recv()
            summed = own[k] + core_in[k].astype(F32)
            if side == 1:
                y_out[z] = summed.astype(BF16)
                y_copy(z).start()
            else:
                own[k] = summed

    def chain(z):
        k = z * p.wide
        if p.wide > 1:
            y_copy(z).wait_recv()
            own[k] = own[k] + y_in[z].astype(F32)

        @pl.when((z >= p.z) & (p.z > 0))
        def _():
            up_copy(z).wait_recv()
            own[k] = own[k] + from_below[z].astype(F32)

        @pl.when((z <= p.z) & (p.z < p.depth - 1))
        def _():
            down_copy(z).wait_recv()
            own[k] = own[k] + from_above[z].astype(F32)

        @pl.when(z != p.z)
        def _():
            z_out[z] = own[k].astype(BF16)

        @pl.when(z > p.z)
        def _():
            up_copy(z).start()

        @pl.when(z < p.z)
        def _():
            down_copy(z).start()

        @pl.when(z == p.z)
        def _():
            out[...] = own[k]

    in_order(compute)
    in_order(pair)
    in_order(chain)

    def drain(z):
        for side in sides:
            core_copy(z, side).wait_send()
        if p.wide > 1:
            y_copy(z).wait_send()

        @pl.when(z != p.z)
        def _():
            up_copy(z).wait_send()

    in_order(drain)


def back(n, left, basis_in):
    features, width = basis_in.shape
    depth, wide = grid_of(n)
    sems = pltpu.SemaphoreType.DMA
    piece = (OUT_ROWS, width)
    return pl.pallas_call(
        functools.partial(back_kernel, n),
        out_shape=jax.ShapeDtypeStruct(piece, F32),
        in_specs=[
            pl.BlockSpec(memory_space=pltpu.VMEM),
            pl.BlockSpec(memory_space=pl.ANY),
        ],
        out_specs=pl.BlockSpec(memory_space=pltpu.VMEM),
        scratch_shapes=[
            pltpu.VMEM((n, width, width), F32),
            pltpu.VMEM((depth * wide, *piece), F32),
            pltpu.VMEM((depth * wide, *piece), BF16),
            pltpu.VMEM((depth * wide, *piece), BF16),
            pltpu.VMEM((depth, *piece), BF16),
            pltpu.VMEM((depth, *piece), BF16),
            pltpu.VMEM((depth, *piece), BF16),
            pltpu.VMEM((depth, *piece), BF16),
            pltpu.VMEM((depth, *piece), BF16),
            sems((n,)),
            sems((depth * wide,)),
            sems((depth * wide,)),
            sems((depth,)),
            sems((depth,)),
            sems((depth,)),
            sems((depth,)),
            sems((depth,)),
        ],
        compiler_params=pltpu.CompilerParams(
            collective_id=1, has_side_effects=True, vmem_limit_bytes=VMEM_BYTES
        ),
        name="back_rotate",
    )(left, basis_in)


def per_device(n, acts, grads, lengths, basis_in, basis_out):
    rows = jnp.concatenate([acts.reshape(ROW_TILE, -1), grads.reshape(ROW_TILE, -1)], 0)
    rot_out, window, rot_in, damp = rotate_all(n, rows, lengths, basis_in, basis_out)
    corrections, left = correct(lengths, rot_out, window, rot_in, damp)
    precond = back(n, left, basis_in)
    return (corrections, precond)


def solution(mesh):
    in_specs = (
        P(("groups", "eigen"), None),
        P(("groups", "eigen"), None),
        P("groups"),
        P("groups", "eigen"),
        P("groups", "eigen"),
    )
    out_specs = (P("groups", "eigen"), P("groups", "eigen"))
    return jax.shard_map(
        functools.partial(per_device, mesh.shape["eigen"]),
        mesh=mesh,
        in_specs=in_specs,
        out_specs=out_specs,
        check_vma=False,
    )
```

```python
import functools

import jax
import jax.numpy as jnp
from jax import lax
from jax.experimental import pallas as pl
from jax.experimental.pallas import tpu as pltpu
from jax.sharding import PartitionSpec as P

SEQS = 4
OUT_ROWS = 128
CORES = 2
ROW_TILE = 16
BANDS = 4
GROUP = 4
damp_share = 0.1
BF16 = jnp.bfloat16
F32 = jnp.float32
VMEM_BYTES = 56 * 1024 * 1024


def grid_of(n):
    wide = 2 if n <= 16 else 1
    return n // (CORES * wide), wide


class Place:
    def __init__(self, n):
        self.n = n
        self.depth, self.wide = grid_of(n)
        self.me = lax.axis_index("eigen")
        self.core = lax.rem(self.me, CORES)
        self.y = lax.rem(self.me // CORES, self.wide)
        self.z = self.me // (CORES * self.wide)

    def at(self, z, y, core):
        return (z * self.wide + y) * CORES + core


def entry_barrier(place):
    barrier = pltpu.get_barrier_semaphore()
    for step in range(1, place.n):
        other = lax.rem(place.me + step, place.n)
        pl.semaphore_signal(
            barrier, inc=1, device_id={"eigen": other}, device_id_type=pl.DeviceIdType.MESH
        )
    pl.semaphore_wait(barrier, place.n - 1)


def remote(src, dst, send_sem, recv_sem, to):
    return pltpu.make_async_remote_copy(
        src_ref=src,
        dst_ref=dst,
        send_sem=send_sem,
        recv_sem=recv_sem,
        device_id={"eigen": to},
        device_id_type=pl.DeviceIdType.MESH,
    )


class Gather:
    def __init__(self, place, slots, send_sems, recv_sems):
        self.p, self.slots = place, slots
        self.send_sems, self.recv_sems = send_sems, recv_sems

    def copy(self, slot, way, to):
        return remote(
            self.slots.at[slot],
            self.slots.at[slot],
            self.send_sems.at[way, slot],
            self.recv_sems.at[slot],
            to,
        )

    def arrived(self, slot):
        self.copy(slot, 0, self.p.at(self.p.z, self.p.y, 1 - self.p.core)).wait_recv()

    def along(self, act):
        p = self.p
        for h in range(p.depth - 1, 0, -1):
            for there in (p.z + h, p.z - h):

                @pl.when((there >= 0) & (there < p.depth))
                def _():
                    act(
                        remote(
                            self.slots.at[p.me],
                            self.slots.at[p.me],
                            self.send_sems.at[0, there],
                            self.recv_sems.at[p.me],
                            p.at(there, p.y, p.core),
                        )
                    )

    def across(self, slot, act):
        p = self.p
        if p.wide > 1:
            act(self.copy(slot, 1, p.at(p.z, 1 - p.y, p.core)))
        self.over(slot, act)

    def over(self, slot, act):
        p = self.p
        act(self.copy(slot, 2, p.at(p.z, p.y, 1 - p.core)))

    def beside(self, dz):
        p = self.p
        if p.wide > 1:
            slot = p.at(p.z + dz, 1 - p.y, p.core)
            self.arrived(slot)
            self.over(slot, start)

    def round(self, h):
        p = self.p
        if h == 0:
            self.along(start)
            self.across(p.me, start)
            return

        @pl.when(p.z - h >= 0)
        def _():
            slot = p.at(p.z - h, p.y, p.core)
            self.arrived(slot)
            self.across(slot, start)

        @pl.when(p.z + h < p.depth)
        def _():
            slot = p.at(p.z + h, p.y, p.core)
            self.arrived(slot)
            self.across(slot, start)

        self.beside_round(h - 1)

    def beside_round(self, h):
        p = self.p
        if h == 0:
            self.beside(0)
            return

        @pl.when(p.z - h >= 0)
        def _():
            self.beside(-h)

        @pl.when(p.z + h < p.depth)
        def _():
            self.beside(h)

    def last(self):
        p = self.p
        self.beside_round(p.depth - 1)
        for z in range(p.depth):
            for y in range(p.wide):
                self.arrived(p.at(z, y, 1 - p.core))

    def drain(self):
        p = self.p
        self.along(wait_send)
        for z in range(p.depth):
            self.across(p.at(z, p.y, p.core), wait_send)
            if p.wide > 1:
                self.over(p.at(z, 1 - p.y, p.core), wait_send)


def start(copy):
    copy.start()


def wait_send(copy):
    copy.wait_send()


def sequence_ends(lengths):
    ends, total = [], 0
    for s in range(SEQS):
        total = total + lengths[s]
        ends.append(total)
    return ends


def sequence_of(position, ends):
    which = jnp.zeros(position.shape, jnp.int32)
    for s in range(SEQS - 1):
        which = which + (position >= ends[s]).astype(jnp.int32)
    return which


def rotate_kernel(
    n,
    acts_ref,
    grads_ref,
    lengths,
    basis_in,
    basis_out,
    rot_out_hbm,
    window_hbm,
    rot_in_ref,
    damp_ref,
    held,
    rows,
    tokens,
    lefts,
    window_f32,
    window,
    rot_out,
    parts,
    acc,
    held_sems,
    token_send,
    token_recv,
    window_send,
    window_recv,
    rot_send,
    rot_recv,
    part_send,
    part_recv,
    local_sems,
):
    place = Place(n)
    features, width = basis_in.shape
    steps = held.shape[1]
    chunk = features // steps
    count = rot_in_ref.shape[0]

    def load(which, k):
        source = basis_out if which == 0 else basis_in
        return pltpu.make_async_copy(
            source.at[pl.ds(k * chunk, chunk)], held.at[which, k], held_sems.at[which, k]
        )

    first_rows = pltpu.make_async_copy(
        basis_out.at[pl.ds(0, OUT_ROWS)], window_f32, local_sems.at[0]
    )
    first_rows.start()
    for which in range(2):
        for k in range(steps):
            load(which, k).start()

    for base, source in ((0, acts_ref), (ROW_TILE, grads_ref)):
        whole = source[...].astype(F32)
        for r in range(ROW_TILE):
            t, k = r // steps, r % steps
            rows[base + r : base + r + 1, :] = whole[t : t + 1, k * chunk : (k + 1) * chunk]
    tokens[place.me] = rows[...].astype(BF16)
    entry_barrier(place)
    token_gather = Gather(place, tokens, token_send, token_recv)
    window_gather = Gather(place, window, window_send, window_recv)
    rot_gather = Gather(place, rot_out, rot_send, rot_recv)
    token_gather.round(0)
    first_rows.wait()
    window[place.me] = window_f32[...].astype(BF16)
    window_gather.along(start)
    for h in range(1, place.depth):
        token_gather.round(h)
    token_gather.last()
    window_gather.across(place.me, start)

    def arrange(which):
        row = lax.broadcasted_iota(jnp.int32, (n * ROW_TILE, n * ROW_TILE), 0)
        col = lax.broadcasted_iota(jnp.int32, (n * ROW_TILE, n * ROW_TILE), 1)
        pick = (col == lax.rem(row, count) * steps + row // count).astype(F32).astype(BF16)
        here = pl.ds((1 - which) * ROW_TILE, ROW_TILE)
        flat = tokens[:, here, :].reshape(n * ROW_TILE, chunk)
        lefts[which] = jnp.dot(pick, flat, preferred_element_type=F32).astype(BF16)

    def rotate(which, low, high):
        for k in range(low, high):
            load(which, k).wait()
            left = lefts[which, k * count : (k + 1) * count, :]
            block = held[which, k]
            high_part = block.astype(BF16)
            low_part = (block - high_part.astype(F32)).astype(BF16)
            acc[...] += jnp.dot(left, high_part, preferred_element_type=F32) + jnp.dot(
                left, low_part, preferred_element_type=F32
            )

    later = list(range(1, place.depth))
    arrange(0)
    acc[...] = jnp.zeros_like(acc)
    rotate(0, 0, steps // 4)
    for h in later[:1]:
        window_gather.round(h)
    rotate(0, steps // 4, steps * 5 // 8)
    for h in later[1:2]:
        window_gather.round(h)
    rotate(0, steps * 5 // 8, steps)
    rot_out[place.me] = acc[...].astype(BF16)
    rot_gather.round(0)
    for h in later[2:]:
        window_gather.round(h)
    arrange(1)
    acc[...] = jnp.zeros_like(acc)
    rotate(1, 0, steps // 2)
    for h in later:
        rot_gather.round(h)
    rotate(1, steps // 2, steps)
    rot_in = acc[...].astype(BF16)
    rot_in_ref[...] = rot_in
    rot_gather.last()

    contract = (((1,), (1,)), ((), ()))
    gram_in = lax.dot_general(rot_in, rot_in, contract, preferred_element_type=F32)
    gram_out = jnp.zeros((count, count), F32)
    for d in range(n):
        gram_out += lax.dot_general(rot_out[d], rot_out[d], contract, preferred_element_type=F32)
    ends = sequence_ends(lengths)
    one = sequence_of(lax.broadcasted_iota(jnp.int32, (count, count), 0), ends)
    two = sequence_of(lax.broadcasted_iota(jnp.int32, (count, count), 1), ends)
    inner = jnp.sum(jnp.where(one == two, gram_in * gram_out, 0.0))
    parts[place.me] = jnp.full(parts.shape[1:], inner, F32)

    def part_copy(step):
        other = lax.rem(place.me + step, n)
        return remote(
            parts.at[place.me],
            parts.at[place.me],
            part_send.at[step],
            part_recv.at[place.me],
            other,
        )

    for step in range(1, n):
        part_copy(step).start()
    out_copy = pltpu.make_async_copy(rot_out, rot_out_hbm, local_sems.at[1])
    out_copy.start()
    window_gather.last()
    window_copy = pltpu.make_async_copy(window, window_hbm, local_sems.at[2])
    window_copy.start()
    for step in range(1, n):
        other = lax.rem(place.me + step, n)
        remote(
            parts.at[other], parts.at[other], part_send.at[step], part_recv.at[other], other
        ).wait_recv()
    total = jnp.sum(parts[...], axis=0)
    damp_ref[...] = total * (damp_share / (SEQS * features * (n * width)))
    for step in range(1, n):
        part_copy(step).wait_send()
    token_gather.drain()
    window_gather.drain()
    rot_gather.drain()
    out_copy.wait()
    window_copy.wait()


def rotate_all(n, acts, grads, lengths, basis_in, basis_out):
    features, width = basis_in.shape
    steps = ROW_TILE // acts.shape[0]
    chunk = features // steps
    count = n * acts.shape[0]
    sems = pltpu.SemaphoreType.DMA
    return pl.pallas_call(
        functools.partial(rotate_kernel, n),
        out_shape=(
            jax.ShapeDtypeStruct((n, count, width), BF16),
            jax.ShapeDtypeStruct((n, OUT_ROWS, width), BF16),
            jax.ShapeDtypeStruct((count, width), BF16),
            jax.ShapeDtypeStruct((8, 128), F32),
        ),
        in_specs=[
            pl.BlockSpec(memory_space=pltpu.VMEM),
            pl.BlockSpec(memory_space=pltpu.VMEM),
            pl.BlockSpec(memory_space=pltpu.SMEM),
            pl.BlockSpec(memory_space=pl.ANY),
            pl.BlockSpec(memory_space=pl.ANY),
        ],
        out_specs=(
            pl.BlockSpec(memory_space=pl.ANY),
            pl.BlockSpec(memory_space=pl.ANY),
            pl.BlockSpec(memory_space=pltpu.VMEM),
            pl.BlockSpec(memory_space=pltpu.VMEM),
        ),
        scratch_shapes=[
            pltpu.VMEM((2, steps, chunk, width), F32),
            pltpu.VMEM((2 * ROW_TILE, chunk), F32),
            pltpu.VMEM((n, 2 * ROW_TILE, chunk), BF16),
            pltpu.VMEM((2, steps * count, chunk), BF16),
            pltpu.VMEM((OUT_ROWS, width), F32),
            pltpu.VMEM((n, OUT_ROWS, width), BF16),
            pltpu.VMEM((n, count, width), BF16),
            pltpu.VMEM((n, 8, 128), F32),
            pltpu.VMEM((count, width), F32),
            sems((2, steps)),
            sems((3, n)),
            sems((n,)),
            sems((3, n)),
            sems((n,)),
            sems((3, n)),
            sems((n,)),
            sems((n,)),
            sems((n,)),
            sems((3,)),
        ],
        compiler_params=pltpu.CompilerParams(
            collective_id=0, has_side_effects=True, vmem_limit_bytes=VMEM_BYTES
        ),
        name="rotate_and_gather",
    )(acts, grads, lengths, basis_in, basis_out)


def correct_kernel(lengths, rot_out, window, rot_in, damp, corrections, left, masked):
    block = pl.program_id(0)
    count, width = rot_in.shape

    @pl.when(block == 0)
    def _():
        which = sequence_of(
            lax.broadcasted_iota(jnp.int32, (count, width), 0), sequence_ends(lengths)
        )
        half = rot_in[...].astype(F32) * 0.5
        for s in range(SEQS):
            masked[:, s * width : (s + 1) * width] = jnp.where(which == s, half, 0.0).astype(BF16)
        left[...] = jnp.zeros_like(left)

    columns = jnp.concatenate(
        [rot_out[g].astype(F32).T.astype(BF16) for g in range(rot_out.shape[0])], 0
    )
    tile = 128
    damping = damp[0:1, 0:1]
    scaled = []
    for low in range(0, columns.shape[0], tile):
        rows = columns[low : low + tile]
        squares, total = None, None
        for s in range(SEQS):
            product = jnp.dot(
                rows, masked[:, s * width : (s + 1) * width], preferred_element_type=F32
            )
            squares = product * product if s == 0 else squares + product * product
            total = product if s == 0 else total + product
        corrections[low : low + tile, :] = squares
        scaled.append((total * pl.reciprocal(squares + damping, approx=True)).astype(BF16))
    per = len(scaled) // rot_out.shape[0]
    for g in range(rot_out.shape[0]):
        left[...] += jnp.dot(
            window[g],
            jnp.concatenate(scaled[g * per : (g + 1) * per], 0),
            preferred_element_type=F32,
        )

    @pl.when(block == pl.num_programs(0) - 1)
    def _():
        left[...] = left[...] * 0.5


def correct(lengths, rot_out, window, rot_in, damp):
    n, count, width = rot_out.shape
    whole = lambda i: (0, 0)
    return pl.pallas_call(
        correct_kernel,
        grid=(n // GROUP,),
        out_shape=(
            jax.ShapeDtypeStruct((n * width, width), F32),
            jax.ShapeDtypeStruct((OUT_ROWS, width), F32),
        ),
        in_specs=[
            pl.BlockSpec(memory_space=pltpu.SMEM),
            pl.BlockSpec((GROUP, count, width), lambda i: (i, 0, 0)),
            pl.BlockSpec((GROUP, OUT_ROWS, width), lambda i: (i, 0, 0)),
            pl.BlockSpec((count, width), whole),
            pl.BlockSpec((8, 128), whole),
        ],
        out_specs=(
            pl.BlockSpec((GROUP * width, width), lambda i: (i, 0)),
            pl.BlockSpec((OUT_ROWS, width), whole),
        ),
        scratch_shapes=[pltpu.VMEM((count, SEQS * width), BF16)],
        compiler_params=pltpu.CompilerParams(vmem_limit_bytes=VMEM_BYTES),
        name="corrections",
    )(lengths, rot_out, window, rot_in, damp)


def back_kernel(
    n,
    left_ref,
    basis,
    out,
    held,
    own,
    core_out,
    core_in,
    y_out,
    y_in,
    z_out,
    z_in,
    held_sems,
    core_send,
    core_recv,
    y_send,
    y_recv,
    z_send,
    z_recv,
):
    place = Place(n)
    p = place
    width = basis.shape[1]

    def load(d):
        return pltpu.make_async_copy(
            basis.at[pl.ds(pl.multiple_of(d * width, width), width)], held.at[d], held_sems.at[d]
        )

    far, near = jnp.maximum(p.z, p.depth - 1 - p.z), jnp.minimum(p.z, p.depth - 1 - p.z)

    def turn(i):
        alone = jnp.where(p.z < p.depth - 1 - p.z, p.depth - 1 - i, i)
        j = jnp.maximum(i - (far - near), 0)
        reach = near - j // 2
        paired = jnp.where(lax.rem(j, 2) == 0, p.z + reach, p.z - reach)
        return jnp.where(i < far - near, alone, paired)

    turns = [turn(i) for i in range(p.depth)]

    def load_all(z):
        for y in range(p.wide):
            for core in range(CORES):
                load(p.at(z, y, core)).start()

    for z in turns:
        load_all(z)
    left = left_ref[...].astype(BF16)
    entry_barrier(place)

    def partial_of(z, y, core):
        d = p.at(z, y, core)
        load(d).wait()
        return lax.dot_general(
            left, held[d].astype(BF16), (((1,), (1,)), ((), ())), preferred_element_type=F32
        )

    sides = [1, 0] if p.wide > 1 else [0]

    def core_copy(z, side):
        k = z * p.wide + side
        return remote(
            core_out.at[k],
            core_in.at[k],
            core_send.at[k],
            core_recv.at[k],
            p.at(p.z, p.y, 1 - p.core),
        )

    def y_copy(z, b):
        return remote(
            y_out.at[z, b],
            y_in.at[z, b],
            y_send.at[z, b],
            y_recv.at[z, b],
            p.at(p.z, 1 - p.y, p.core),
        )

    def z_copy(source, z, b):
        return remote(
            z_out.at[z, b],
            z_in.at[source, b],
            z_send.at[z, b],
            z_recv.at[source, b],
            p.at(z, p.y, p.core),
        )

    part = OUT_ROWS // BANDS

    def band(b):
        return pl.ds(b * part, part)

    def compute(z):
        for side in sides:
            y = 1 - p.y if side == 1 else p.y
            core_out[z * p.wide + side] = partial_of(z, y, 1 - p.core).astype(BF16)
            core_copy(z, side).start()
        for side in sides:
            y = 1 - p.y if side == 1 else p.y
            own[z * p.wide + side] = partial_of(z, y, p.core)

    def pair(z):
        for side in sides:
            k = z * p.wide + side
            core_copy(z, side).wait_recv()
            for b in range(BANDS):
                summed = own[k, band(b), :] + core_in[k, band(b), :].astype(F32)
                if side == 1:
                    y_out[z, b] = summed.astype(BF16)
                    y_copy(z, b).start()
                else:
                    own[k, band(b), :] = summed

    def chain(z):
        k = z * p.wide
        for b in range(BANDS):
            rows = band(b)
            if p.wide > 1:
                y_copy(z, b).wait_recv()
                own[k, rows, :] = own[k, rows, :] + y_in[z, b].astype(F32)

            @pl.when(z != p.z)
            def _():
                z_out[z, b] = own[k, rows, :].astype(BF16)
                z_copy(p.z, z, b).start()

    def finish():
        k = p.z * p.wide
        for b in range(BANDS):
            rows = band(b)
            for z in range(p.depth):

                @pl.when(z != p.z)
                def _():
                    z_copy(z, z, b).wait_recv()
                    own[k, rows, :] = own[k, rows, :] + z_in[z, b].astype(F32)

            out[rows, :] = own[k, rows, :]

    for i in range(p.depth + 2):
        if i < p.depth:
            compute(turns[i])
        if 1 <= i <= p.depth:
            pair(turns[i - 1])
        if i >= 2:
            chain(turns[i - 2])
    finish()

    for z in range(p.depth):
        for side in sides:
            core_copy(z, side).wait_send()
        for b in range(BANDS):
            if p.wide > 1:
                y_copy(z, b).wait_send()

            @pl.when(z != p.z)
            def _():
                z_copy(p.z, z, b).wait_send()


def back(n, left, basis_in):
    features, width = basis_in.shape
    depth, wide = grid_of(n)
    sems = pltpu.SemaphoreType.DMA
    piece = (OUT_ROWS, width)
    bands = (depth, BANDS, OUT_ROWS // BANDS, width)
    return pl.pallas_call(
        functools.partial(back_kernel, n),
        out_shape=jax.ShapeDtypeStruct(piece, F32),
        in_specs=[
            pl.BlockSpec(memory_space=pltpu.VMEM),
            pl.BlockSpec(memory_space=pl.ANY),
        ],
        out_specs=pl.BlockSpec(memory_space=pltpu.VMEM),
        scratch_shapes=[
            pltpu.VMEM((n, width, width), F32),
            pltpu.VMEM((depth * wide, *piece), F32),
            pltpu.VMEM((depth * wide, *piece), BF16),
            pltpu.VMEM((depth * wide, *piece), BF16),
            pltpu.VMEM(bands, BF16),
            pltpu.VMEM(bands, BF16),
            pltpu.VMEM(bands, BF16),
            pltpu.VMEM(bands, BF16),
            sems((n,)),
            sems((depth * wide,)),
            sems((depth * wide,)),
            sems((depth, BANDS)),
            sems((depth, BANDS)),
            sems((depth, BANDS)),
            sems((depth, BANDS)),
        ],
        compiler_params=pltpu.CompilerParams(
            collective_id=1, has_side_effects=True, vmem_limit_bytes=VMEM_BYTES
        ),
        name="back_rotate",
    )(left, basis_in)


def per_device(n, acts, grads, lengths, basis_in, basis_out):
    rot_out, window, rot_in, damp = rotate_all(n, acts, grads, lengths, basis_in, basis_out)
    corrections, left = correct(lengths, rot_out, window, rot_in, damp)
    precond = back(n, left, basis_in)
    return (corrections, precond)


def solution(mesh):
    in_specs = (
        P(("groups", "eigen"), None),
        P(("groups", "eigen"), None),
        P("groups"),
        P("groups", "eigen"),
        P("groups", "eigen"),
    )
    out_specs = (P("groups", "eigen"), P("groups", "eigen"))
    return jax.shard_map(
        functools.partial(per_device, mesh.shape["eigen"]),
        mesh=mesh,
        in_specs=in_specs,
        out_specs=out_specs,
        check_vma=False,
    )
```
